256 devices in a mesh: rep: 16 (over x, z_lo), seq: 16 (over z_hi, y, core).
Axes of the slice: x: 4, y: 4, z: 8 (z_hi: 2, z_lo: 4; z = z_hi * 4 + z_lo), core: 2. Of those that a mesh axis runs over, the one named last changes fastest.
Arguments:
- tokens: bfloat16 [16, 1536, 5120], P('rep', 'seq'), may hold values from -6 to 6
- steps: int32 [16], P('rep'), may hold values from 0 to 49
- counts: int32 [16], P('rep'), may hold values from 768 to 1536, as said below
- mod_base: float32 [2, 5120], replicated, may hold values from -3 to 3
- mod_time: float32 [2, 5120], replicated, may hold values from -3 to 3
- w_query: float32 [5120, 4096], P('rep', 'seq')
- w_key: float32 [5120, 4096], P('rep', 'seq')
- w_value: float32 [5120, 4096], P('rep', 'seq'), may hold values from -0.078125 to 0.078125
Outputs:
- attended: bfloat16 [16, 1536, 4096], P('rep', 'seq')
The draws below stay inside these ranges and needn't reach their ends.
Inputs may be any that keep to these rules, and one draw needn't show every extreme that they name: Keys at positions counts[r] or later are padding; some replica has all 1536 tokens valid.
All inputs are finite; a program needn't handle non-finite values.
Results may differ from the reference program's by a relative error of at most 0.015.
The reference program's roundings to bfloat16 on the way (of `modulated` and `probs`) count: a program that leaves them out, or rounds other values in their place, can miss the bound.
Values may be sent and summed in bfloat16 or wider, within the bound.
No kernel may reach another device: no remote copies, remote signals or barrier semaphores. Data moves between devices by JAX's collectives and lax.ppermute only.
A program may use at most 128 MiB of HBM per device.

```python
import math
import jax
import jax.numpy as jnp
from jax import lax

D = 5120
HEAD = 128
STEPS = 50
INNER = 4096
TOKENS = 1536
REPLICAS = 16


def shared_rows(key):
    return jax.random.normal(key, (D, INNER), jnp.float32) * D ** (-0.5)


def draw_w_key(key, part):
    base_rows = shared_rows(key)
    return base_rows


def draw_w_query(key, part):
    key = jax.random.fold_in(key, 7)
    own_rows = jax.random.normal(key, (D, INNER), jnp.float32) * D ** (-0.5)
    return own_rows


def draw_counts(key, part):
    key = jax.random.fold_in(key, 3)
    first_key, second_key = jax.random.split(key)
    drawn = jax.random.randint(first_key, (REPLICAS,), TOKENS // 2, TOKENS + 1)
    position = jax.random.randint(second_key, (), 0, REPLICAS)
    return drawn.at[position].set(TOKENS).astype(jnp.int32)


def plant(values, key, least, high):
    dims = values.shape
    index_at = [jax.random.randint(jax.random.fold_in(key, axis), (), 0, dims[axis]) for axis in range(len(dims))]
    values = values.at[tuple(index_at)].set(least)
    longest = dims.index(max(dims))
    index_at[longest] = (index_at[longest] + 1) % dims[longest]
    return values.at[tuple(index_at)].set(high)


def shard_levels(stream_key, extent, shards, least, top_value):
    loudness = 1.0
    for axis_at, blocks in shards:
        heights = jax.random.uniform(jax.random.fold_in(jax.random.fold_in(stream_key, 6), axis_at), (blocks,), jnp.float32, least / len(shards), top_value / len(shards))
        loudness = loudness * jnp.repeat(jnp.exp(heights), extent[axis_at] // blocks).reshape((-1,) + (1,) * (len(extent) - 1 - axis_at))
    return loudness


def normal_values(key, shape, scale, reach, shards=(), kind=jnp.bfloat16):
    gain = shard_levels(key, shape, shards, -0.22, 0.18) if shards else 1.0
    values = jax.random.normal(key, shape, jnp.float32) * scale * gain
    return jnp.minimum(jnp.maximum(values, -reach), reach).astype(kind)


def setup_inputs(seed: int = 0) -> dict:
    key_list = jax.random.split(jax.random.key(seed), 9)
    return {
        "tokens": normal_values(key_list[0], (REPLICAS, TOKENS, D), 1.0, 6.0, ((0, 16), (1, 16))),
        "steps": plant(jax.random.randint(key_list[1], (REPLICAS,), 0, STEPS), jax.random.fold_in(key_list[1], 1), 0, STEPS - 1).astype(jnp.int32),
        "counts": draw_counts(jax.random.fold_in(key_list[8], 71), 0),
        "mod_base": normal_values(key_list[3], (2, D), 0.5, 3.0, (), jnp.float32),
        "mod_time": normal_values(key_list[4], (2, D), 0.5, 3.0, (), jnp.float32),
        "w_query": draw_w_query(jax.random.fold_in(key_list[8], 71), 0),
        "w_key": draw_w_key(jax.random.fold_in(key_list[8], 71), 0),
        "w_value": normal_values(key_list[7], (D, INNER), D ** -0.5, 0.078125, ((0, 16), (1, 16)), jnp.float32),
    }


def modulation(step_value, mod_base, mod_time, width):
    frac = 1.0 - step_value.astype(jnp.float32) / STEPS
    sigma = 5.0 * frac / (1.0 + 4.0 * frac)
    half_width = width // 2
    freqs = jnp.exp(-math.log(10000.0) * jnp.arange(half_width, dtype=jnp.float32) / half_width)
    angles = 1000.0 * sigma * freqs
    embedding = jnp.concatenate([jnp.cos(angles), jnp.sin(angles)])
    return (mod_base[0] + mod_time[0] * embedding, mod_base[1] + mod_time[1] * embedding)

def modulate(token_rows, shift_row, scale_row):
    values = token_rows.astype(jnp.float32)
    center = lax.optimization_barrier(jnp.mean(values, axis=1, keepdims=True))
    spread = lax.optimization_barrier(jnp.mean((values - center) ** 2, axis=1, keepdims=True))
    normed = (values - center) * lax.rsqrt(spread + 1e-06)
    return (normed * (1.0 + scale_row) + shift_row).astype(jnp.bfloat16)

def attend(query, keys, values, valid_count):
    total = query.shape[0]
    head_count = query.shape[1] // HEAD
    block_size = min(512, total)
    query3 = query.reshape(total // block_size, block_size, head_count, HEAD)
    keys3 = keys.reshape(total, head_count, HEAD).astype(jnp.float32)
    values3 = values.reshape(total, head_count, HEAD).astype(jnp.float32)
    valid = jnp.arange(total) < valid_count

    def one_block(query_block):
        scores = jnp.einsum('qhd,khd->hqk', query_block.astype(jnp.float32), keys3) / math.sqrt(HEAD)
        scores = jnp.where(valid[None, None, :], scores, -1e+30)
        top = lax.optimization_barrier(jnp.max(scores, axis=2, keepdims=True))
        weights = jnp.exp(scores - top)
        probs = (weights / lax.optimization_barrier(jnp.sum(weights, axis=2, keepdims=True))).astype(jnp.bfloat16)
        result = jnp.einsum('hqk,khd->qhd', probs.astype(jnp.float32), values3)
        return result.reshape(block_size, head_count * HEAD).astype(jnp.bfloat16)
    return lax.map(one_block, query3).reshape(total, head_count * HEAD)

def reference(tokens, steps, counts, mod_base, mod_time, w_query, w_key, w_value):
    wq = w_query.astype(jnp.bfloat16)
    wk = w_key.astype(jnp.bfloat16)
    wv = w_value.astype(jnp.bfloat16)
    outputs = []
    for replica in range(REPLICAS):
        shift_row, scale_row = modulation(steps[replica], mod_base, mod_time, D)
        modulated = modulate(tokens[replica], shift_row, scale_row)
        query = jnp.dot(modulated, wq, preferred_element_type=jnp.float32).astype(jnp.bfloat16)
        keys = jnp.dot(modulated, wk, preferred_element_type=jnp.float32).astype(jnp.bfloat16)
        values = jnp.dot(modulated, wv, preferred_element_type=jnp.float32).astype(jnp.bfloat16)
        outputs.append(attend(query, keys, values, counts[replica]))
    return jnp.stack(outputs)
```

```python
import functools
import math

import jax
import jax.numpy as jnp
from jax import lax
from jax.experimental import pallas as pl
from jax.experimental.pallas import tpu as pltpu
from jax.sharding import PartitionSpec as P

HEAD = 128
STEPS = 50

ZL = 4
NX = 4
NY = 4
NC = 2


def rep_perm(move):
    pairs = []
    for x in range(NX):
        for z in range(ZL):
            goal = move(x, z)
            if goal is not None:
                pairs.append((x * ZL + z, (goal[0] % NX) * ZL + goal[1]))
    return pairs


def seq_perm(move):
    pairs = []
    for h in range(2):
        for y in range(NY):
            for c in range(NC):
                a, b, d = move(h, y, c)
                pairs.append(((h * NY + y) * NC + c, (a * NY + b % NY) * NC + d))
    return pairs


X_UP = rep_perm(lambda x, z: (x + 1, z))
X_DOWN = rep_perm(lambda x, z: (x - 1, z))
Z_PAIR = rep_perm(lambda x, z: (x, z ^ 1))
Z_MIDDLE = rep_perm(lambda x, z: (x, 3 - z) if z in (1, 2) else None)
Z_OUTER = rep_perm(lambda x, z: (x, z ^ 1) if z in (1, 2) else None)
H_SWAP = seq_perm(lambda h, y, c: (1 - h, y, c))
Y_UP = seq_perm(lambda h, y, c: (h, y + 1, c))
Y_DOWN = seq_perm(lambda h, y, c: (h, y - 1, c))
C_SWAP = seq_perm(lambda h, y, c: (h, y, 1 - c))


def modulation(step_value, mod_base, mod_time, width):
    frac = 1.0 - step_value.astype(jnp.float32) / STEPS
    sigma = 5.0 * frac / (1.0 + 4.0 * frac)
    half_width = width // 2
    freqs = jnp.exp(-math.log(10000.0) * jnp.arange(half_width, dtype=jnp.float32) / half_width)
    angles = 1000.0 * sigma * freqs
    embedding = jnp.concatenate([jnp.cos(angles), jnp.sin(angles)])
    return (mod_base[0] + mod_time[0] * embedding, mod_base[1] + mod_time[1] * embedding)


def cast_kernel(q_ref, k_ref, v_ref, out_ref):
    width = q_ref.shape[1]
    out_ref[:, :width] = q_ref[...].astype(jnp.bfloat16)
    out_ref[:, width : 2 * width] = k_ref[...].astype(jnp.bfloat16)
    out_ref[:, 2 * width :] = v_ref[...].astype(jnp.bfloat16)


def cast_weights(w_query, w_key, w_value):
    rows, width = w_query.shape
    return pl.pallas_call(
        cast_kernel,
        out_shape=jax.ShapeDtypeStruct((rows, 3 * width), jnp.bfloat16),
        name="cast_weights",
    )(w_query, w_key, w_value)


def modulate_kernel(rows_ref, shift_ref, scale_ref, low_ref, high_ref):
    half = low_ref.shape[0]
    for at, out_ref in ((0, low_ref), (half, high_ref)):
        values = rows_ref[0, at : at + half, :].astype(jnp.float32)
        center = jnp.mean(values, axis=1, keepdims=True)
        moved = values - center
        spread = jnp.mean(moved * moved, axis=1, keepdims=True)
        normed = moved * lax.rsqrt(spread + 1e-06)
        out_ref[...] = (normed * (1.0 + scale_ref[...]) + shift_ref[...]).astype(jnp.bfloat16)


def modulate(tokens, shift_row, scale_row):
    _, rows, width = tokens.shape
    half = jax.ShapeDtypeStruct((rows // 2, width), jnp.bfloat16)
    return pl.pallas_call(
        modulate_kernel,
        out_shape=(half, half),
        name="modulate",
    )(tokens, shift_row[None], scale_row[None])


def after(arrays, *others):
    count = len(arrays)
    return lax.optimization_barrier(tuple(arrays) + tuple(others))[:count]


def attend_kernel(count_ref, place_ref, *refs, heads, n_tokens, n_weights):
    token_refs = refs[:n_tokens]
    weight_refs = refs[n_tokens : n_tokens + n_weights]
    out_ref, x_ref, w_ref, qkv_ref, v_ref, token_sem, weight_sem = refs[n_tokens + n_weights :]
    total = x_ref.shape[0]
    rows = token_refs[0].shape[0]
    depth = weight_refs[0].shape[0]
    copies = []
    for i, ref in enumerate(weight_refs):
        at = pl.multiple_of(place_ref[n_tokens + i] * depth, depth)
        copies.append(pltpu.make_async_copy(ref, w_ref.at[pl.ds(at, depth), :], weight_sem.at[i]))
    for i, ref in enumerate(token_refs):
        at = pl.multiple_of(place_ref[i] * rows, rows)
        copies.append(pltpu.make_async_copy(ref, x_ref.at[pl.ds(at, rows), :], token_sem.at[i]))
    for copy in copies:
        copy.start()
    for copy in copies:
        copy.wait()

    tile = 256
    width = qkv_ref.shape[1] // 3

    @pl.loop(0, total // tile)
    def _(step):
        at = pl.ds(pl.multiple_of(step * tile, tile), tile)
        for n in range(3):
            cols = slice(n * width, (n + 1) * width)
            qkv_ref[at, cols] = jnp.dot(
                x_ref[at, :], w_ref[:, cols], preferred_element_type=jnp.float32
            ).astype(jnp.bfloat16)

    valid = lax.broadcasted_iota(jnp.int32, (total, HEAD), 0) < count_ref[0]
    for head in range(heads):
        keys_at = slice(width + head * HEAD, width + (head + 1) * HEAD)
        values_at = slice(2 * width + head * HEAD, 2 * width + (head + 1) * HEAD)
        first_key = qkv_ref[0:1, keys_at].astype(jnp.float32)
        qkv_ref[:, keys_at] = jnp.where(
            valid, qkv_ref[:, keys_at].astype(jnp.float32), first_key
        ).astype(jnp.bfloat16)
        values = qkv_ref[:, values_at].astype(jnp.float32)
        v_ref[head, :, :HEAD] = jnp.where(valid, values, 0.0).astype(jnp.bfloat16)
        v_ref[head, :, HEAD:] = jnp.where(valid, 1.0, 0.0).astype(jnp.bfloat16)

    factor = math.log2(math.e) / math.sqrt(HEAD)
    for head in range(heads):
        keys_at = slice(width + head * HEAD, width + (head + 1) * HEAD)

        @pl.loop(0, total // tile)
        def _(step):
            at = pl.ds(pl.multiple_of(step * tile, tile), tile)
            query = qkv_ref[at, head * HEAD : (head + 1) * HEAD]
            scores = lax.dot_general(
                query, qkv_ref[:, keys_at], (((1,), (1,)), ((), ())), preferred_element_type=jnp.float32
            )
            top = jnp.max(scores, axis=1, keepdims=True)
            weights = jnp.exp2((scores - top) * factor).astype(jnp.bfloat16)
            result = jnp.dot(weights, v_ref[head], preferred_element_type=jnp.float32)
            out_ref[at, head * HEAD : (head + 1) * HEAD] = (
                result[:, :HEAD] / result[:, HEAD : HEAD + 1]
            ).astype(jnp.bfloat16)


def project_and_attend(count, places, token_blocks, weight_blocks):
    rows, width = token_blocks[0].shape
    total = rows * len(token_blocks)
    columns = weight_blocks[0].shape[1]
    heads = columns // 3 // HEAD
    smem = pl.BlockSpec(memory_space=pltpu.SMEM)
    anywhere = pl.BlockSpec(memory_space=pl.ANY)
    return pl.pallas_call(
        functools.partial(
            attend_kernel, heads=heads, n_tokens=len(token_blocks), n_weights=len(weight_blocks)
        ),
        out_shape=jax.ShapeDtypeStruct((total, heads * HEAD), jnp.bfloat16),
        in_specs=[smem, smem] + [anywhere] * (len(token_blocks) + len(weight_blocks)),
        out_specs=pl.BlockSpec(memory_space=pltpu.VMEM),
        scratch_shapes=[
            pltpu.VMEM((total, width), jnp.bfloat16),
            pltpu.VMEM((width, columns), jnp.bfloat16),
            pltpu.VMEM((total, columns), jnp.bfloat16),
            pltpu.VMEM((heads, total, 2 * HEAD), jnp.bfloat16),
            pltpu.SemaphoreType.DMA((len(token_blocks),)),
            pltpu.SemaphoreType.DMA((len(weight_blocks),)),
        ],
        compiler_params=pltpu.CompilerParams(vmem_limit_bytes=56 * 1024 * 1024),
        name="project_and_attend",
    )(count, places, *token_blocks, *weight_blocks)


def shards(tokens, steps, counts, mod_base, mod_time, w_query, w_key, w_value):
    width = tokens.shape[2]
    rep, seq = lax.axis_index("rep"), lax.axis_index("seq")
    x_at, z_at = rep // ZL, rep % ZL
    h_at, y_at, c_at = seq // (NY * NC), (seq // NC) % NY, seq % NC

    def rep_send(block, perm):
        return lax.ppermute(block, "rep", perm)

    def seq_send(block, perm):
        return lax.ppermute(block, "seq", perm)

    own = cast_weights(w_query, w_key, w_value)
    pair = rep_send(own, Z_PAIR)
    middle0 = rep_send(own, Z_MIDDLE)
    own_up, own_down = rep_send(own, X_UP), rep_send(own, X_DOWN)

    shift_row, scale_row = modulation(steps[0], mod_base, mod_time, width)
    t0, t1 = modulate(tokens, shift_row, scale_row)
    z0, z1 = seq_send(t0, H_SWAP), seq_send(t1, H_SWAP)
    t0_up, t1_down = seq_send(t0, Y_UP), seq_send(t1, Y_DOWN)
    t0_down, t1_up = seq_send(t0, Y_DOWN), seq_send(t1, Y_UP)
    t0_c, t1_c = seq_send(t0, C_SWAP), seq_send(t1, C_SWAP)

    middle1 = rep_send(pair, Z_MIDDLE)
    pair_up, pair_down = rep_send(pair, X_UP), rep_send(pair, X_DOWN)
    own_far = rep_send(own_up, X_UP)

    t0_far, t1_far = seq_send(t0_up, Y_UP), seq_send(t1_down, Y_DOWN)

    (z0,) = after((z0,), t0_up, t1_down)
    z0_up, z0_down = seq_send(z0, Y_UP), seq_send(z0, Y_DOWN)
    first = [(t0_up, 0, -1, 0), (t1_up, 0, -1, 1), (t0_down, 0, 1, 0), (t1_down, 0, 1, 1), (z0, 1, 0, 0)]

    outer0 = rep_send(middle0, Z_OUTER)
    outer1 = rep_send(middle1, Z_OUTER)
    inner = (z_at == 1) | (z_at == 2)
    far0 = jnp.where(inner, middle0, outer0)
    far1 = jnp.where(inner, middle1, outer1)
    pair_far = rep_send(pair_down, X_DOWN)
    far0_up, far0_down = rep_send(far0, X_UP), rep_send(far0, X_DOWN)

    (z1,) = after((z1,), z0, t0_far, t1_far)
    z1_up, z1_down = seq_send(z1, Y_UP), seq_send(z1, Y_DOWN)
    z0_far = seq_send(z0_up, Y_UP)
    far0_far = rep_send(far0_up, X_UP)
    far1_up, far1_down = rep_send(far1, X_UP), rep_send(far1, X_DOWN)
    z1_far = seq_send(z1_down, Y_DOWN)
    far1_far = rep_send(far1_down, X_DOWN)

    mine = [(t0, 0, 0, 0), (t1, 0, 0, 1)] + first + [
        (t0_far, 0, 2, 0), (t1_far, 0, 2, 1), (z1, 1, 0, 1),
        (z0_up, 1, -1, 0), (z0_down, 1, 1, 0), (z1_up, 1, -1, 1), (z1_down, 1, 1, 1),
        (z0_far, 1, 2, 0), (z1_far, 1, 2, 1),
    ]
    blocks, places = [], []
    for block, other, hop, part in mine:
        base = (h_at ^ other) * NY + (y_at + hop) % NY
        if block is t0 or block is t1:
            sent = t0_c if block is t0 else t1_c
        else:
            sent = seq_send(block, C_SWAP)
        blocks += [block, sent]
        places += [(base * NC + c_at) * 2 + part, (base * NC + 1 - c_at) * 2 + part]

    slots = [z_at, z_at ^ 1, jnp.where(z_at < 2, 2, 1), jnp.where(z_at < 2, 3, 0)]
    weights = []
    for z_place, group in zip(slots, (
        (own, own_up, own_down, own_far), (pair, pair_up, pair_down, pair_far),
        (far0, far0_up, far0_down, far0_far), (far1, far1_up, far1_down, far1_far),
    )):
        for hop, block in zip((0, -1, 1, 2), group):
            weights.append(block)
            places.append(((x_at + hop) % NX) * ZL + z_place)
    head_output = project_and_attend(
        counts, jnp.stack(places).astype(jnp.int32), blocks, weights
    )
    attended = lax.all_to_all(head_output, "seq", split_axis=0, concat_axis=1, tiled=True)
    return attended[None]


def solution(mesh):
    in_specs = (
        P("rep", "seq", None),
        P("rep"),
        P("rep"),
        P(),
        P(),
        P("rep", "seq"),
        P("rep", "seq"),
        P("rep", "seq"),
    )
    out_specs = P("rep", "seq", None)
    return jax.shard_map(shards, mesh=mesh, in_specs=in_specs, out_specs=out_specs, check_vma=False)
```

```python
import functools
import math

import jax
import jax.numpy as jnp
from jax import lax
from jax.experimental import pallas as pl
from jax.experimental.pallas import tpu as pltpu
from jax.sharding import PartitionSpec as P

HEAD = 128
STEPS = 50
EARLY = 64
SPACE = 15 * 1024 + 512

ZL = 4
NX = 4
NY = 4
NC = 2


def rep_perm(move):
    pairs = []
    for x in range(NX):
        for z in range(ZL):
            goal = move(x, z)
            if goal is not None:
                pairs.append((x * ZL + z, (goal[0] % NX) * ZL + goal[1]))
    return pairs


def seq_perm(move):
    pairs = []
    for h in range(2):
        for y in range(NY):
            for c in range(NC):
                a, b, d = move(h, y, c)
                pairs.append(((h * NY + y) * NC + c, (a * NY + b % NY) * NC + d))
    return pairs


X_UP = rep_perm(lambda x, z: (x + 1, z))
X_DOWN = rep_perm(lambda x, z: (x - 1, z))
Z_PAIR = rep_perm(lambda x, z: (x, z ^ 1))
Z_MIDDLE = rep_perm(lambda x, z: (x, 3 - z) if z in (1, 2) else None)
Z_OUTER = rep_perm(lambda x, z: (x, z ^ 1) if z in (1, 2) else None)
H_SWAP = seq_perm(lambda h, y, c: (1 - h, y, c))
Y_UP = seq_perm(lambda h, y, c: (h, y + 1, c))
Y_DOWN = seq_perm(lambda h, y, c: (h, y - 1, c))
C_SWAP = seq_perm(lambda h, y, c: (h, y, 1 - c))


def modulation(step_value, mod_base, mod_time, width):
    frac = 1.0 - step_value.astype(jnp.float32) / STEPS
    sigma = 5.0 * frac / (1.0 + 4.0 * frac)
    half_width = width // 2
    freqs = jnp.exp(-math.log(10000.0) * jnp.arange(half_width, dtype=jnp.float32) / half_width)
    angles = 1000.0 * sigma * freqs
    embedding = jnp.concatenate([jnp.cos(angles), jnp.sin(angles)])
    return (mod_base[0] + mod_time[0] * embedding, mod_base[1] + mod_time[1] * embedding)


def cast_kernel(q_ref, k_ref, v_ref, before_ref, out_ref):
    width = q_ref.shape[1]
    for n, ref in enumerate((q_ref, k_ref, v_ref)):
        low = ref[...].astype(jnp.bfloat16)
        out_ref[:, n * width : (n + 1) * width] = low


def cast_weights(w_query, w_key, w_value, before):
    rows, width = w_query.shape
    shape = jax.ShapeDtypeStruct((rows, 3 * width), jnp.bfloat16)
    return pl.pallas_call(
        cast_kernel,
        out_shape=shape,
        in_specs=[pl.BlockSpec(memory_space=pltpu.VMEM)] * 3 + [pl.BlockSpec(memory_space=pl.ANY)],
        name="cast_weights",
    )(w_query, w_key, w_value, before)


def modulate_kernel(rows_ref, shift_ref, scale_ref, all_ref, early_ref, late_ref):
    values = rows_ref[0].astype(jnp.float32)
    center = jnp.mean(values, axis=1, keepdims=True)
    moved = values - center
    spread = jnp.mean(moved * moved, axis=1, keepdims=True)
    normed = moved * lax.rsqrt(spread + 1e-06)
    result = (normed * (1.0 + scale_ref[...]) + shift_ref[...]).astype(jnp.bfloat16)
    early = early_ref.shape[0]
    all_ref[...] = result
    early_ref[...] = result[:early]
    late_ref[...] = result[early:]


def modulate(tokens, shift_row, scale_row, early):
    _, rows, width = tokens.shape
    return pl.pallas_call(
        modulate_kernel,
        out_shape=tuple(
            jax.ShapeDtypeStruct((count, width), jnp.bfloat16) for count in (rows, early, rows - early)
        ),
        name="modulate",
    )(tokens, shift_row[None], scale_row[None])


def gate_kernel(*refs):
    pass


class Order:
    def __init__(self, first):
        self.last = first
        self.flying = {}

    def gate(self, array, before=None):
        anywhere = pl.BlockSpec(memory_space=pl.ANY)
        others = [self.last] if before is None else [self.last, before]
        self.last = pl.pallas_call(
            gate_kernel,
            out_shape=jax.ShapeDtypeStruct(array.shape, array.dtype),
            in_specs=[anywhere] * (1 + len(others)),
            out_specs=anywhere,
            input_output_aliases={0: 0},
            scratch_shapes=[pltpu.VMEM((SPACE, 1024), jnp.float32)],
            compiler_params=pltpu.CompilerParams(vmem_limit_bytes=63 * 1024 * 1024),
            name="gate",
        )(array, *others)
        return self.last

    def start(self, name, array, axis, perm):
        self.flying[name] = lax.ppermute(array, axis, perm)

    def finish(self, name, before=None):
        return self.gate(self.flying.pop(name), before)


def load_weights(place_ref, first, weight_refs, w_ref, sem):
    depth = weight_refs[0].shape[0]
    copies = []
    for i, ref in enumerate(weight_refs):
        at = pl.multiple_of(place_ref[first + i] * depth, depth)
        copies.append(pltpu.make_async_copy(ref, w_ref.at[pl.ds(at, depth), :], sem.at[i]))
    return copies


def attend_kernel(count_ref, place_ref, near_ref, *refs, heads, pieces, n_tokens, n_weights):
    token_refs = refs[:n_tokens]
    weight_refs = refs[n_tokens : n_tokens + n_weights]
    out_ref, x_ref, w_ref, qkv_ref, k_ref, v_ref, near_sem, x_sem, w_sem = refs[n_tokens + n_weights :]
    half = near_ref.shape[0]
    tile = 256
    w_copies = load_weights(place_ref, 1 + len(pieces), weight_refs, w_ref, w_sem)
    near_copies = [
        pltpu.make_async_copy(near_ref.at[pl.ds(at, tile), :], x_ref.at[pl.ds(at, tile), :], near_sem.at[at // tile])
        for at in range(0, half, tile)
    ]
    x_copies = []
    for i, (source, first, rows) in enumerate(pieces):
        at = pl.multiple_of(half + place_ref[1 + i] * 16, 16)
        x_copies.append(
            pltpu.make_async_copy(
                token_refs[source].at[pl.ds(first, rows), :], x_ref.at[pl.ds(at, rows), :], x_sem.at[i]
            )
        )
    for copy in w_copies + near_copies[:1]:
        copy.start()
    for copy in w_copies:
        copy.wait()
    for copy in near_copies[1:] + x_copies:
        copy.start()
    for at in range(0, 2 * half, tile):
        if at < half:
            near_copies[at // tile].wait()
        elif at == half:
            for copy in x_copies:
                copy.wait()
        qkv_ref[at : at + tile, :] = jnp.dot(
            x_ref[at : at + tile, :], w_ref[...], preferred_element_type=jnp.float32
        ).astype(jnp.bfloat16)

    place = place_ref[0]
    width = heads * HEAD
    rows_at = lax.broadcasted_iota(jnp.int32, (half, HEAD), 0)
    for part in range(2):
        h_place = place if part == 0 else 1 - place
        valid = rows_at + h_place * half < count_ref[0]
        to = slice(part * half, (part + 1) * half)
        for head in range(heads):
            cols = slice(head * HEAD, (head + 1) * HEAD)
            keys_at = slice(width + head * HEAD, width + (head + 1) * HEAD)
            values_at = slice(2 * width + head * HEAD, 2 * width + (head + 1) * HEAD)
            first_key = jnp.where(
                place == 0,
                qkv_ref[0:1, keys_at].astype(jnp.float32),
                qkv_ref[half : half + 1, keys_at].astype(jnp.float32),
            )
            keys = qkv_ref[to, keys_at].astype(jnp.float32)
            k_ref[to, cols] = jnp.where(valid, keys, first_key).astype(jnp.bfloat16)
            values = qkv_ref[to, values_at].astype(jnp.float32)
            v_ref[head, to, :HEAD] = jnp.where(valid, values, 0.0).astype(jnp.bfloat16)
            v_ref[head, to, HEAD:] = jnp.where(valid, 1.0, 0.0).astype(jnp.bfloat16)

    factor = math.log2(math.e) / math.sqrt(HEAD)
    steps = half // tile

    @pl.loop(0, 2 * steps)
    def _(step):
        at = pl.ds(pl.multiple_of(step * tile, tile), tile)
        to = pl.ds(pl.multiple_of(((step + place * steps) % (2 * steps)) * tile, tile), tile)
        for head in range(heads):
            cols = slice(head * HEAD, (head + 1) * HEAD)
            scores = lax.dot_general(
                qkv_ref[at, cols], k_ref[:, cols], (((1,), (1,)), ((), ())), preferred_element_type=jnp.float32
            )
            top = jnp.max(scores, axis=1, keepdims=True)
            weights = jnp.exp2((scores - top) * factor).astype(jnp.bfloat16)
            result = jnp.dot(weights, v_ref[head], preferred_element_type=jnp.float32)
            out_ref[to, cols] = (result[:, :HEAD] / result[:, HEAD : HEAD + 1]).astype(jnp.bfloat16)


def attend_all(count, places, near, pieces, tokens, weight_blocks):
    half, width = near.shape
    columns = weight_blocks[0].shape[1]
    heads = columns // 3 // HEAD
    smem = pl.BlockSpec(memory_space=pltpu.SMEM)
    vmem = pl.BlockSpec(memory_space=pltpu.VMEM)
    anywhere = pl.BlockSpec(memory_space=pl.ANY)
    return pl.pallas_call(
        functools.partial(
            attend_kernel, heads=heads, pieces=pieces, n_tokens=len(tokens), n_weights=len(weight_blocks)
        ),
        out_shape=jax.ShapeDtypeStruct((2 * half, heads * HEAD), jnp.bfloat16),
        in_specs=[smem, smem] + [anywhere] * (1 + len(tokens) + len(weight_blocks)),
        out_specs=vmem,
        scratch_shapes=[
            pltpu.VMEM((2 * half, width), jnp.bfloat16),
            pltpu.VMEM((width, columns), jnp.bfloat16),
            pltpu.VMEM((2 * half, columns), jnp.bfloat16),
            pltpu.VMEM((2 * half, heads * HEAD), jnp.bfloat16),
            pltpu.VMEM((heads, 2 * half, 2 * HEAD), jnp.bfloat16),
            pltpu.SemaphoreType.DMA((half // 256,)),
            pltpu.SemaphoreType.DMA((len(pieces),)),
            pltpu.SemaphoreType.DMA((len(weight_blocks),)),
        ],
        compiler_params=pltpu.CompilerParams(vmem_limit_bytes=56 * 1024 * 1024),
        name="attend_all",
    )(count, places, near, *tokens, *weight_blocks)


def shards(tokens, steps, counts, mod_base, mod_time, w_query, w_key, w_value):
    width = tokens.shape[2]
    rep, seq = lax.axis_index("rep"), lax.axis_index("seq")
    x_at, z_at = rep // ZL, rep % ZL
    h_at, y_at, c_at = seq // (NY * NC), (seq // NC) % NY, seq % NC

    rows = tokens.shape[1]
    early, late = EARLY, rows - EARLY
    shift_row, scale_row = modulation(steps[0], mod_base, mod_time, width)
    mine, t0, t1 = modulate(tokens, shift_row, scale_row, early)
    groups = [[(h * NY + y) * NC + c for y in range(NY) for c in range(NC)] for h in range(2)]
    near = lax.all_gather(mine, "seq", axis=0, axis_index_groups=groups, tiled=True)
    own = cast_weights(w_query, w_key, w_value, mine)

    inner = (z_at == 1) | (z_at == 2)
    order = Order(own)
    order.start("z0", t0, "seq", H_SWAP)
    order.start("own_u", own, "rep", X_UP)
    order.start("own_d", own, "rep", X_DOWN)
    order.start("pair", own, "rep", Z_PAIR)
    order.start("mid0", own, "rep", Z_MIDDLE)
    own_u = order.finish("own_u")
    order.start("own_f", own_u, "rep", X_UP)
    own_d = order.finish("own_d")
    pair = order.finish("pair")
    order.start("mid1", pair, "rep", Z_MIDDLE)
    order.start("pair_u", pair, "rep", X_UP)
    order.start("pair_d", pair, "rep", X_DOWN)
    mid0 = order.finish("mid0")
    order.start("out0", mid0, "rep", Z_OUTER)
    z0 = order.finish("z0")
    away = lax.all_gather(z0, "seq", axis=0, axis_index_groups=groups, tiled=True)
    mid1 = order.finish("mid1")
    order.start("out1", mid1, "rep", Z_OUTER)
    own_f = order.finish("own_f")
    far0 = jnp.where(inner, mid0, order.finish("out0"))
    pair_u = order.finish("pair_u")
    order.start("far0_u", far0, "rep", X_UP)
    pair_d = order.finish("pair_d")
    order.start("far0_d", far0, "rep", X_DOWN)
    order.start("pair_f", pair_d, "rep", X_DOWN)
    far1 = jnp.where(inner, mid1, order.finish("out1", near))
    order.start("z1", order.gate(t1), "seq", H_SWAP)
    far0_u = order.finish("far0_u")
    order.start("far1_u", far1, "rep", X_UP)
    order.start("far0_f", far0_u, "rep", X_UP)
    far0_d = order.finish("far0_d")
    order.start("far1_d", far1, "rep", X_DOWN)
    pair_f = order.finish("pair_f")
    far1_u = order.finish("far1_u")
    far1_d = order.finish("far1_d")
    order.start("far1_f", far1_d, "rep", X_DOWN)
    far0_f = order.finish("far0_f")
    z1 = order.finish("z1")
    order.start("z1_u", z1, "seq", Y_UP)
    order.start("z1_d", z1, "seq", Y_DOWN)
    order.start("z1_c", z1, "seq", C_SWAP)
    z1_d = order.finish("z1_d")
    order.start("z1_f", z1_d, "seq", Y_DOWN)
    order.start("z1_dc", z1_d, "seq", C_SWAP)
    z1_u = order.finish("z1_u")
    order.start("z1_uc", z1_u, "seq", C_SWAP)
    far1_f = order.finish("far1_f")
    z1_f = order.finish("z1_f")
    order.start("z1_fc", z1_f, "seq", C_SWAP)
    z1_c, z1_dc, z1_uc, z1_fc = [order.flying.pop(name) for name in ("z1_c", "z1_dc", "z1_uc", "z1_fc")]

    slots = [z_at, z_at ^ 1, jnp.where(z_at < 2, 2, 1), jnp.where(z_at < 2, 3, 0)]
    weights, w_places = [], []
    for z_place, group in zip(slots, (
        (own, own_u, own_d, own_f), (pair, pair_u, pair_d, pair_f),
        (far0, far0_u, far0_d, far0_f), (far1, far1_u, far1_d, far1_f),
    )):
        for hop, block in zip((0, -1, 1, 2), group):
            weights.append(block)
            w_places.append(((x_at + hop) % NX) * ZL + z_place)
    w_places = jnp.stack(w_places).astype(jnp.int32)
    blocks = [away, z1, z1_c, z1_u, z1_uc, z1_d, z1_dc, z1_f, z1_fc]
    unit = rows // 16
    pieces, places = [], [h_at]
    for i in range(NY * NC):
        pieces.append((0, i * early, early))
        places.append(jnp.int32(i * unit))
    for hop in (0, -1, 1, 2):
        for other in range(2):
            pieces.append((len(pieces) - NY * NC + 1, 0, late))
            places.append((((y_at + hop) % NY) * NC + (c_at ^ other)) * unit + early // 16)
    places = jnp.concatenate([jnp.stack(places).astype(jnp.int32), w_places])
    head_output = attend_all(counts, places, near, pieces, blocks, weights)
    attended = lax.all_to_all(head_output, "seq", split_axis=0, concat_axis=1, tiled=True)
    return attended[None]


def solution(mesh):
    in_specs = (
        P("rep", "seq", None),
        P("rep"),
        P("rep"),
        P(),
        P(),
        P("rep", "seq"),
        P("rep", "seq"),
        P("rep", "seq"),
    )
    out_specs = P("rep", "seq", None)
    return jax.shard_map(shards, mesh=mesh, in_specs=in_specs, out_specs=out_specs, check_vma=False)
```

```python
import functools
import math

import jax
import jax.numpy as jnp
from jax import lax
from jax.experimental import pallas as pl
from jax.experimental.pallas import tpu as pltpu
from jax.sharding import PartitionSpec as P

HEAD = 128
STEPS = 50
EARLY = 64
SPACE = 15 * 1024 + 512

ZL = 4
NX = 4
NY = 4
NC = 2


def rep_perm(move):
    pairs = []
    for x in range(NX):
        for z in range(ZL):
            goal = move(x, z)
            if goal is not None:
                pairs.append((x * ZL + z, (goal[0] % NX) * ZL + goal[1]))
    return pairs


def seq_perm(move):
    pairs = []
    for h in range(2):
        for y in range(NY):
            for c in range(NC):
                a, b, d = move(h, y, c)
                pairs.append(((h * NY + y) * NC + c, (a * NY + b % NY) * NC + d))
    return pairs


X_UP = rep_perm(lambda x, z: (x + 1, z))
X_DOWN = rep_perm(lambda x, z: (x - 1, z))
Z_PAIR = rep_perm(lambda x, z: (x, z ^ 1))
Z_MIDDLE = rep_perm(lambda x, z: (x, 3 - z) if z in (1, 2) else None)
Z_OUTER = rep_perm(lambda x, z: (x, z ^ 1) if z in (1, 2) else None)
H_SWAP = seq_perm(lambda h, y, c: (1 - h, y, c))
Y_UP = seq_perm(lambda h, y, c: (h, y + 1, c))
Y_DOWN = seq_perm(lambda h, y, c: (h, y - 1, c))
C_SWAP = seq_perm(lambda h, y, c: (h, y, 1 - c))


def modulation(step_value, mod_base, mod_time, width):
    frac = 1.0 - step_value.astype(jnp.float32) / STEPS
    sigma = 5.0 * frac / (1.0 + 4.0 * frac)
    half_width = width // 2
    freqs = jnp.exp(-math.log(10000.0) * jnp.arange(half_width, dtype=jnp.float32) / half_width)
    angles = 1000.0 * sigma * freqs
    embedding = jnp.concatenate([jnp.cos(angles), jnp.sin(angles)])
    return (mod_base[0] + mod_time[0] * embedding, mod_base[1] + mod_time[1] * embedding)


def cast_kernel(q_ref, k_ref, v_ref, before_ref, out_ref):
    width = q_ref.shape[1]
    for n, ref in enumerate((q_ref, k_ref, v_ref)):
        low = ref[...].astype(jnp.bfloat16)
        out_ref[:, n * width : (n + 1) * width] = low


def cast_weights(w_query, w_key, w_value, before):
    rows, width = w_query.shape
    shape = jax.ShapeDtypeStruct((rows, 3 * width), jnp.bfloat16)
    return pl.pallas_call(
        cast_kernel,
        out_shape=shape,
        in_specs=[pl.BlockSpec(memory_space=pltpu.VMEM)] * 3 + [pl.BlockSpec(memory_space=pl.ANY)],
        name="cast_weights",
    )(w_query, w_key, w_value, before)


def modulate_kernel(rows_ref, shift_ref, scale_ref, all_ref, early_ref, late_ref):
    values = rows_ref[0].astype(jnp.float32)
    center = jnp.mean(values, axis=1, keepdims=True)
    moved = values - center
    spread = jnp.mean(moved * moved, axis=1, keepdims=True)
    normed = moved * lax.rsqrt(spread + 1e-06)
    result = (normed * (1.0 + scale_ref[...]) + shift_ref[...]).astype(jnp.bfloat16)
    early = early_ref.shape[0]
    all_ref[...] = result
    early_ref[...] = result[:early]
    late_ref[...] = result[early:]


def modulate(tokens, shift_row, scale_row, early):
    _, rows, width = tokens.shape
    return pl.pallas_call(
        modulate_kernel,
        out_shape=tuple(
            jax.ShapeDtypeStruct((count, width), jnp.bfloat16) for count in (rows, early, rows - early)
        ),
        name="modulate",
    )(tokens, shift_row[None], scale_row[None])


def gate_kernel(*refs):
    pass


class Order:
    def __init__(self, first):
        self.last = first
        self.flying = {}

    def gate(self, array, before=None):
        anywhere = pl.BlockSpec(memory_space=pl.ANY)
        others = [self.last] if before is None else [self.last, before]
        self.last = pl.pallas_call(
            gate_kernel,
            out_shape=jax.ShapeDtypeStruct(array.shape, array.dtype),
            in_specs=[anywhere] * (1 + len(others)),
            out_specs=anywhere,
            input_output_aliases={0: 0},
            scratch_shapes=[pltpu.VMEM((SPACE, 1024), jnp.float32)],
            compiler_params=pltpu.CompilerParams(vmem_limit_bytes=63 * 1024 * 1024),
            name="gate",
        )(array, *others)
        return self.last

    def start(self, name, array, axis, perm):
        self.flying[name] = lax.ppermute(array, axis, perm)

    def finish(self, name, before=None):
        return self.gate(self.flying.pop(name), before)


def load_weights(place_ref, first, weight_refs, w_ref, sem):
    depth = weight_refs[0].shape[0]
    copies = []
    for i, ref in enumerate(weight_refs):
        at = pl.multiple_of(place_ref[first + i] * depth, depth)
        copies.append(pltpu.make_async_copy(ref, w_ref.at[pl.ds(at, depth), :], sem.at[i]))
    return copies


def attend_kernel(count_ref, place_ref, near_ref, *refs, heads, pieces, n_tokens, n_weights):
    token_refs = refs[:n_tokens]
    weight_refs = refs[n_tokens : n_tokens + n_weights]
    out_ref, x_ref, w_ref, qkv_ref, k_ref, v_ref, near_sem, x_sem, w_sem = refs[n_tokens + n_weights :]
    half = near_ref.shape[0]
    tile = 256
    w_copies = load_weights(place_ref, 1 + len(pieces), weight_refs, w_ref, w_sem)
    near_copies = [
        pltpu.make_async_copy(near_ref.at[pl.ds(at, tile), :], x_ref.at[pl.ds(at, tile), :], near_sem.at[at // tile])
        for at in range(0, half, tile)
    ]
    x_copies = []
    for i, (source, first, rows) in enumerate(pieces):
        at = pl.multiple_of(half + place_ref[1 + i] * 16, 16)
        x_copies.append(
            pltpu.make_async_copy(
                token_refs[source].at[pl.ds(first, rows), :], x_ref.at[pl.ds(at, rows), :], x_sem.at[i]
            )
        )
    for copy in w_copies + near_copies[:1]:
        copy.start()
    for copy in w_copies:
        copy.wait()
    for copy in near_copies[1:] + x_copies:
        copy.start()
    for at in range(0, 2 * half, tile):
        if at < half:
            near_copies[at // tile].wait()
        elif at == half:
            for copy in x_copies:
                copy.wait()
        qkv_ref[at : at + tile, :] = jnp.dot(
            x_ref[at : at + tile, :], w_ref[...], preferred_element_type=jnp.float32
        ).astype(jnp.bfloat16)

    place = place_ref[0]
    width = heads * HEAD
    rows_at = lax.broadcasted_iota(jnp.int32, (half, HEAD), 0)
    for part in range(2):
        h_place = place if part == 0 else 1 - place
        valid = rows_at + h_place * half < count_ref[0]
        to = slice(part * half, (part + 1) * half)
        for head in range(heads):
            cols = slice(head * HEAD, (head + 1) * HEAD)
            keys_at = slice(width + head * HEAD, width + (head + 1) * HEAD)
            values_at = slice(2 * width + head * HEAD, 2 * width + (head + 1) * HEAD)
            first_key = jnp.where(
                place == 0,
                qkv_ref[0:1, keys_at].astype(jnp.float32),
                qkv_ref[half : half + 1, keys_at].astype(jnp.float32),
            )
            keys = qkv_ref[to, keys_at].astype(jnp.float32)
            k_ref[to, cols] = jnp.where(valid, keys, first_key).astype(jnp.bfloat16)
            values = qkv_ref[to, values_at].astype(jnp.float32)
            v_ref[head, to, :HEAD] = jnp.where(valid, values, 0.0).astype(jnp.bfloat16)
            v_ref[head, to, HEAD:] = jnp.where(valid, 1.0, 0.0).astype(jnp.bfloat16)

    factor = math.log2(math.e) / math.sqrt(HEAD)
    steps = half // tile

    @pl.loop(0, 2 * steps)
    def _(step):
        at = pl.ds(pl.multiple_of(step * tile, tile), tile)
        to = pl.ds(pl.multiple_of(((step + place * steps) % (2 * steps)) * tile, tile), tile)
        for head in range(heads):
            cols = slice(head * HEAD, (head + 1) * HEAD)
            scores = lax.dot_general(
                qkv_ref[at, cols], k_ref[:, cols], (((1,), (1,)), ((), ())), preferred_element_type=jnp.float32
            )
            top = jnp.max(scores, axis=1, keepdims=True)
            weights = jnp.exp2((scores - top) * factor).astype(jnp.bfloat16)
            result = jnp.dot(weights, v_ref[head], preferred_element_type=jnp.float32)
            out_ref[to, cols] = (result[:, :HEAD] / result[:, HEAD : HEAD + 1]).astype(jnp.bfloat16)


def attend_all(count, places, near, pieces, tokens, weight_blocks):
    half, width = near.shape
    columns = weight_blocks[0].shape[1]
    heads = columns // 3 // HEAD
    smem = pl.BlockSpec(memory_space=pltpu.SMEM)
    vmem = pl.BlockSpec(memory_space=pltpu.VMEM)
    anywhere = pl.BlockSpec(memory_space=pl.ANY)
    return pl.pallas_call(
        functools.partial(
            attend_kernel, heads=heads, pieces=pieces, n_tokens=len(tokens), n_weights=len(weight_blocks)
        ),
        out_shape=jax.ShapeDtypeStruct((2 * half, heads * HEAD), jnp.bfloat16),
        in_specs=[smem, smem] + [anywhere] * (1 + len(tokens) + len(weight_blocks)),
        out_specs=vmem,
        scratch_shapes=[
            pltpu.VMEM((2 * half, width), jnp.bfloat16),
            pltpu.VMEM((width, columns), jnp.bfloat16),
            pltpu.VMEM((2 * half, columns), jnp.bfloat16),
            pltpu.VMEM((2 * half, heads * HEAD), jnp.bfloat16),
            pltpu.VMEM((heads, 2 * half, 2 * HEAD), jnp.bfloat16),
            pltpu.SemaphoreType.DMA((half // 256,)),
            pltpu.SemaphoreType.DMA((len(pieces),)),
            pltpu.SemaphoreType.DMA((len(weight_blocks),)),
        ],
        compiler_params=pltpu.CompilerParams(vmem_limit_bytes=56 * 1024 * 1024),
        name="attend_all",
    )(count, places, near, *tokens, *weight_blocks)


def shards(tokens, steps, counts, mod_base, mod_time, w_query, w_key, w_value):
    width = tokens.shape[2]
    rep, seq = lax.axis_index("rep"), lax.axis_index("seq")
    x_at, z_at = rep // ZL, rep % ZL
    h_at, y_at, c_at = seq // (NY * NC), (seq // NC) % NY, seq % NC

    rows = tokens.shape[1]
    early, late = EARLY, rows - EARLY
    shift_row, scale_row = modulation(steps[0], mod_base, mod_time, width)
    mine, t0, t1 = modulate(tokens, shift_row, scale_row, early)
    groups = [[(h * NY + y) * NC + c for y in range(NY) for c in range(NC)] for h in range(2)]
    near = lax.all_gather(mine, "seq", axis=0, axis_index_groups=groups, tiled=True)
    own = cast_weights(w_query, w_key, w_value, mine)

    inner = (z_at == 1) | (z_at == 2)
    order = Order(own)
    order.start("z0", t0, "seq", H_SWAP)
    order.start("own_u", own, "rep", X_UP)
    order.start("own_d", own, "rep", X_DOWN)
    order.start("pair", own, "rep", Z_PAIR)
    order.start("mid0", own, "rep", Z_MIDDLE)
    own_u = order.finish("own_u")
    order.start("own_f", own_u, "rep", X_UP)
    own_d = order.finish("own_d")
    own_f = order.finish("own_f")
    pair = order.finish("pair")
    order.start("mid1", pair, "rep", Z_MIDDLE)
    order.start("pair_u", pair, "rep", X_UP)
    order.start("pair_d", pair, "rep", X_DOWN)
    mid0 = order.finish("mid0")
    order.start("out0", mid0, "rep", Z_OUTER)
    z0 = order.finish("z0")
    away = lax.all_gather(z0, "seq", axis=0, axis_index_groups=groups, tiled=True)
    mid1 = order.finish("mid1")
    order.start("out1", mid1, "rep", Z_OUTER)
    pair_u = order.finish("pair_u")
    order.start("pair_f", pair_u, "rep", X_UP)
    far0 = jnp.where(inner, mid0, order.finish("out0"))
    order.start("far0_u", far0, "rep", X_UP)
    pair_d = order.finish("pair_d")
    order.start("far0_d", far0, "rep", X_DOWN)
    far1 = jnp.where(inner, mid1, order.finish("out1", near))
    order.start("z1", order.gate(t1), "seq", H_SWAP)
    order.start("far1_d", far1, "rep", X_DOWN)
    pair_f = order.finish("pair_f")
    order.start("far1_u", far1, "rep", X_UP)
    far0_u = order.finish("far0_u")
    far0_d = order.finish("far0_d")
    order.start("far0_f", far0_d, "rep", X_DOWN)
    z1 = order.finish("z1")
    order.start("z1_u", z1, "seq", Y_UP)
    order.start("z1_d", z1, "seq", Y_DOWN)
    far1_u = order.finish("far1_u")
    order.start("far1_f", far1_u, "rep", X_UP)
    far1_d = order.finish("far1_d")
    order.start("z1_c", z1, "seq", C_SWAP)
    far0_f = order.finish("far0_f")
    z1_c = order.finish("z1_c")
    z1_d = order.finish("z1_d")
    order.start("z1_f", z1_d, "seq", Y_DOWN)
    order.start("z1_dc", z1_d, "seq", C_SWAP)
    z1_u = order.finish("z1_u")
    order.start("z1_uc", z1_u, "seq", C_SWAP)
    far1_f = order.finish("far1_f")
    z1_f = order.finish("z1_f")
    order.start("z1_fc", z1_f, "seq", C_SWAP)
    z1_dc, z1_uc, z1_fc = [order.flying.pop(name) for name in ("z1_dc", "z1_uc", "z1_fc")]

    slots = [z_at, z_at ^ 1, jnp.where(z_at < 2, 2, 1), jnp.where(z_at < 2, 3, 0)]
    weights, w_places = [], []
    for z_place, group in zip(slots, (
        (own, own_u, own_d, own_f), (pair, pair_u, pair_d, pair_f),
        (far0, far0_u, far0_d, far0_f), (far1, far1_u, far1_d, far1_f),
    )):
        for hop, block in zip((0, -1, 1, 2), group):
            weights.append(block)
            w_places.append(((x_at + hop) % NX) * ZL + z_place)
    w_places = jnp.stack(w_places).astype(jnp.int32)
    blocks = [away, z1, z1_c, z1_u, z1_uc, z1_d, z1_dc, z1_f, z1_fc]
    unit = rows // 16
    pieces, places = [], [h_at]
    for i in range(NY * NC):
        pieces.append((0, i * early, early))
        places.append(jnp.int32(i * unit))
    for hop in (0, -1, 1, 2):
        for other in range(2):
            pieces.append((len(pieces) - NY * NC + 1, 0, late))
            places.append((((y_at + hop) % NY) * NC + (c_at ^ other)) * unit + early // 16)
    places = jnp.concatenate([jnp.stack(places).astype(jnp.int32), w_places])
    head_output = attend_all(counts, places, near, pieces, blocks, weights)
    attended = lax.all_to_all(head_output, "seq", split_axis=0, concat_axis=1, tiled=True)
    return attended[None]


def solution(mesh):
    in_specs = (
        P("rep", "seq", None),
        P("rep"),
        P("rep"),
        P(),
        P(),
        P("rep", "seq"),
        P("rep", "seq"),
        P("rep", "seq"),
    )
    out_specs = P("rep", "seq", None)
    return jax.shard_map(shards, mesh=mesh, in_specs=in_specs, out_specs=out_specs, check_vma=False)
```

```python
import functools
import math

import jax
import jax.numpy as jnp
from jax import lax
from jax.experimental import pallas as pl
from jax.experimental.pallas import tpu as pltpu
from jax.sharding import PartitionSpec as P

HEAD = 128
STEPS = 50
EARLY = 64
SPACE = 15 * 1024 + 512

ZL = 4
NX = 4
NY = 4
NC = 2


def rep_perm(move):
    pairs = []
    for x in range(NX):
        for z in range(ZL):
            goal = move(x, z)
            if goal is not None:
                pairs.append((x * ZL + z, (goal[0] % NX) * ZL + goal[1]))
    return pairs


def seq_perm(move):
    pairs = []
    for h in range(2):
        for y in range(NY):
            for c in range(NC):
                a, b, d = move(h, y, c)
                pairs.append(((h * NY + y) * NC + c, (a * NY + b % NY) * NC + d))
    return pairs


X_UP = rep_perm(lambda x, z: (x + 1, z))
X_DOWN = rep_perm(lambda x, z: (x - 1, z))
Z_PAIR = rep_perm(lambda x, z: (x, z ^ 1))
Z_MIDDLE = rep_perm(lambda x, z: (x, 3 - z) if z in (1, 2) else None)
Z_OUTER = rep_perm(lambda x, z: (x, z ^ 1) if z in (1, 2) else None)
H_SWAP = seq_perm(lambda h, y, c: (1 - h, y, c))
Y_UP = seq_perm(lambda h, y, c: (h, y + 1, c))
Y_DOWN = seq_perm(lambda h, y, c: (h, y - 1, c))
C_SWAP = seq_perm(lambda h, y, c: (h, y, 1 - c))


def time_embedding(step_value, width):
    frac = 1.0 - step_value.astype(jnp.float32) / STEPS
    sigma = 5.0 * frac / (1.0 + 4.0 * frac)
    half_width = width // 2
    freqs = jnp.exp(-math.log(10000.0) * jnp.arange(half_width, dtype=jnp.float32) / half_width)
    angles = 1000.0 * sigma * freqs
    return jnp.concatenate([jnp.cos(angles), jnp.sin(angles)])


def cast_kernel(q_ref, k_ref, v_ref, before_ref, out_ref):
    width = q_ref.shape[1]
    for n, ref in enumerate((q_ref, k_ref, v_ref)):
        low = ref[...].astype(jnp.bfloat16)
        out_ref[:, n * width : (n + 1) * width] = low


def cast_weights(w_query, w_key, w_value, before):
    rows, width = w_query.shape
    shape = jax.ShapeDtypeStruct((rows, 3 * width), jnp.bfloat16)
    return pl.pallas_call(
        cast_kernel,
        out_shape=shape,
        in_specs=[pl.BlockSpec(memory_space=pltpu.VMEM)] * 3 + [pl.BlockSpec(memory_space=pl.ANY)],
        name="cast_weights",
    )(w_query, w_key, w_value, before)


def modulate_kernel(rows_ref, base_ref, time_ref, embedding_ref, all_ref, early_ref, late_ref):
    embedding = embedding_ref[...]
    shift = base_ref[0:1, :] + time_ref[0:1, :] * embedding
    scale = base_ref[1:2, :] + time_ref[1:2, :] * embedding
    values = rows_ref[0].astype(jnp.float32)
    center = jnp.mean(values, axis=1, keepdims=True)
    moved = values - center
    spread = jnp.mean(moved * moved, axis=1, keepdims=True)
    normed = moved * lax.rsqrt(spread + 1e-06)
    result = (normed * (1.0 + scale) + shift).astype(jnp.bfloat16)
    early = early_ref.shape[0]
    all_ref[...] = result
    early_ref[...] = result[:early]
    late_ref[...] = result[early:]


def modulate(tokens, mod_base, mod_time, embedding, early):
    _, rows, width = tokens.shape
    return pl.pallas_call(
        modulate_kernel,
        out_shape=tuple(
            jax.ShapeDtypeStruct((count, width), jnp.bfloat16) for count in (rows, early, rows - early)
        ),
        name="modulate",
    )(tokens, mod_base, mod_time, embedding[None])


def gate_kernel(*refs):
    pass


class Order:
    def __init__(self, first):
        self.last = first
        self.flying = {}

    def gate(self, array, before=None):
        anywhere = pl.BlockSpec(memory_space=pl.ANY)
        others = [self.last] if before is None else [self.last, before]
        self.last = pl.pallas_call(
            gate_kernel,
            out_shape=jax.ShapeDtypeStruct(array.shape, array.dtype),
            in_specs=[anywhere] * (1 + len(others)),
            out_specs=anywhere,
            input_output_aliases={0: 0},
            scratch_shapes=[pltpu.VMEM((SPACE, 1024), jnp.float32)],
            compiler_params=pltpu.CompilerParams(vmem_limit_bytes=63 * 1024 * 1024),
            name="gate",
        )(array, *others)
        return self.last

    def start(self, name, array, axis, perm):
        self.flying[name] = lax.ppermute(array, axis, perm)

    def finish(self, name, before=None):
        return self.gate(self.flying.pop(name), before)


def load_weights(place_ref, first, weight_refs, w_ref, sem):
    depth = weight_refs[0].shape[0]
    copies = []
    for i, ref in enumerate(weight_refs):
        at = pl.multiple_of(place_ref[first + i] * depth, depth)
        copies.append(pltpu.make_async_copy(ref, w_ref.at[pl.ds(at, depth), :], sem.at[i]))
    return copies


def attend_kernel(count_ref, place_ref, near_ref, *refs, heads, pieces, n_tokens, n_weights):
    token_refs = refs[:n_tokens]
    weight_refs = refs[n_tokens : n_tokens + n_weights]
    out_ref, x_ref, w_ref, qkv_ref, k_ref, v_ref, near_sem, x_sem, w_sem = refs[n_tokens + n_weights :]
    half = near_ref.shape[0]
    tile = 256
    w_copies = load_weights(place_ref, 1 + len(pieces), weight_refs, w_ref, w_sem)
    near_copies = [
        pltpu.make_async_copy(near_ref.at[pl.ds(at, tile), :], x_ref.at[pl.ds(at, tile), :], near_sem.at[at // tile])
        for at in range(0, half, tile)
    ]
    x_copies = []
    for i, (source, first, rows) in enumerate(pieces):
        at = pl.multiple_of(half + place_ref[1 + i] * 16, 16)
        x_copies.append(
            pltpu.make_async_copy(
                token_refs[source].at[pl.ds(first, rows), :], x_ref.at[pl.ds(at, rows), :], x_sem.at[i]
            )
        )
    for copy in w_copies + near_copies[:1]:
        copy.start()
    for copy in w_copies:
        copy.wait()
    for copy in near_copies[1:] + x_copies:
        copy.start()
    for at in range(0, 2 * half, tile):
        if at < half:
            near_copies[at // tile].wait()
        elif at == half:
            for copy in x_copies:
                copy.wait()
        qkv_ref[at : at + tile, :] = jnp.dot(
            x_ref[at : at + tile, :], w_ref[...], preferred_element_type=jnp.float32
        ).astype(jnp.bfloat16)

    place = place_ref[0]
    width = heads * HEAD
    rows_at = lax.broadcasted_iota(jnp.int32, (half, HEAD), 0)
    for part in range(2):
        h_place = place if part == 0 else 1 - place
        valid = rows_at + h_place * half < count_ref[0]
        to = slice(part * half, (part + 1) * half)
        for head in range(heads):
            cols = slice(head * HEAD, (head + 1) * HEAD)
            keys_at = slice(width + head * HEAD, width + (head + 1) * HEAD)
            values_at = slice(2 * width + head * HEAD, 2 * width + (head + 1) * HEAD)
            first_key = jnp.where(
                place == 0,
                qkv_ref[0:1, keys_at].astype(jnp.float32),
                qkv_ref[half : half + 1, keys_at].astype(jnp.float32),
            )
            keys = qkv_ref[to, keys_at].astype(jnp.float32)
            k_ref[to, cols] = jnp.where(valid, keys, first_key).astype(jnp.bfloat16)
            values = qkv_ref[to, values_at].astype(jnp.float32)
            v_ref[head, to, :HEAD] = jnp.where(valid, values, 0.0).astype(jnp.bfloat16)
            v_ref[head, to, HEAD:] = jnp.where(valid, 1.0, 0.0).astype(jnp.bfloat16)

    factor = math.log2(math.e) / math.sqrt(HEAD)
    steps = half // tile

    @pl.loop(0, 2 * steps)
    def _(step):
        at = pl.ds(pl.multiple_of(step * tile, tile), tile)
        to = pl.ds(pl.multiple_of(((step + place * steps) % (2 * steps)) * tile, tile), tile)
        for head in range(heads):
            cols = slice(head * HEAD, (head + 1) * HEAD)
            scores = lax.dot_general(
                qkv_ref[at, cols], k_ref[:, cols], (((1,), (1,)), ((), ())), preferred_element_type=jnp.float32
            )
            top = jnp.max(scores, axis=1, keepdims=True)
            weights = jnp.exp2((scores - top) * factor).astype(jnp.bfloat16)
            result = jnp.dot(weights, v_ref[head], preferred_element_type=jnp.float32)
            out_ref[to, cols] = (result[:, :HEAD] / result[:, HEAD : HEAD + 1]).astype(jnp.bfloat16)


def attend_all(count, places, near, pieces, tokens, weight_blocks):
    half, width = near.shape
    columns = weight_blocks[0].shape[1]
    heads = columns // 3 // HEAD
    smem = pl.BlockSpec(memory_space=pltpu.SMEM)
    vmem = pl.BlockSpec(memory_space=pltpu.VMEM)
    anywhere = pl.BlockSpec(memory_space=pl.ANY)
    return pl.pallas_call(
        functools.partial(
            attend_kernel, heads=heads, pieces=pieces, n_tokens=len(tokens), n_weights=len(weight_blocks)
        ),
        out_shape=jax.ShapeDtypeStruct((2 * half, heads * HEAD), jnp.bfloat16),
        in_specs=[smem, smem] + [anywhere] * (1 + len(tokens) + len(weight_blocks)),
        out_specs=vmem,
        scratch_shapes=[
            pltpu.VMEM((2 * half, width), jnp.bfloat16),
            pltpu.VMEM((width, columns), jnp.bfloat16),
            pltpu.VMEM((2 * half, columns), jnp.bfloat16),
            pltpu.VMEM((2 * half, heads * HEAD), jnp.bfloat16),
            pltpu.VMEM((heads, 2 * half, 2 * HEAD), jnp.bfloat16),
            pltpu.SemaphoreType.DMA((half // 256,)),
            pltpu.SemaphoreType.DMA((len(pieces),)),
            pltpu.SemaphoreType.DMA((len(weight_blocks),)),
        ],
        compiler_params=pltpu.CompilerParams(vmem_limit_bytes=56 * 1024 * 1024),
        name="attend_all",
    )(count, places, near, *tokens, *weight_blocks)


def shards(tokens, steps, counts, mod_base, mod_time, w_query, w_key, w_value):
    width = tokens.shape[2]
    rep, seq = lax.axis_index("rep"), lax.axis_index("seq")
    x_at, z_at = rep // ZL, rep % ZL
    h_at, y_at, c_at = seq // (NY * NC), (seq // NC) % NY, seq % NC

    rows = tokens.shape[1]
    early, late = EARLY, rows - EARLY
    embedding = time_embedding(steps[0], width)
    mine, t0, t1 = modulate(tokens, mod_base, mod_time, embedding, early)
    groups = [[(h * NY + y) * NC + c for y in range(NY) for c in range(NC)] for h in range(2)]
    near = lax.all_gather(mine, "seq", axis=0, axis_index_groups=groups, tiled=True)
    own = cast_weights(w_query, w_key, w_value, mine)

    inner = (z_at == 1) | (z_at == 2)
    order = Order(own)
    order.start("z0", t0, "seq", H_SWAP)
    order.start("own_u", own, "rep", X_UP)
    order.start("own_d", own, "rep", X_DOWN)
    order.start("pair", own, "rep", Z_PAIR)
    order.start("mid0", own, "rep", Z_MIDDLE)
    own_u = order.finish("own_u")
    order.start("own_f", own_u, "rep", X_UP)
    own_d = order.finish("own_d")
    own_f = order.finish("own_f")
    pair = order.finish("pair")
    order.start("mid1", pair, "rep", Z_MIDDLE)
    order.start("pair_u", pair, "rep", X_UP)
    order.start("pair_d", pair, "rep", X_DOWN)
    mid0 = order.finish("mid0")
    order.start("out0", mid0, "rep", Z_OUTER)
    z0 = order.finish("z0")
    away = lax.all_gather(z0, "seq", axis=0, axis_index_groups=groups, tiled=True)
    mid1 = order.finish("mid1")
    order.start("out1", mid1, "rep", Z_OUTER)
    pair_u = order.finish("pair_u")
    order.start("pair_f", pair_u, "rep", X_UP)
    far0 = jnp.where(inner, mid0, order.finish("out0"))
    order.start("far0_u", far0, "rep", X_UP)
    pair_d = order.finish("pair_d")
    order.start("far0_d", far0, "rep", X_DOWN)
    far1 = jnp.where(inner, mid1, order.finish("out1", near))
    order.start("z1", order.gate(t1), "seq", H_SWAP)
    order.start("far1_d", far1, "rep", X_DOWN)
    pair_f = order.finish("pair_f")
    order.start("far1_u", far1, "rep", X_UP)
    far0_u = order.finish("far0_u")
    far0_d = order.finish("far0_d")
    order.start("far0_f", far0_d, "rep", X_DOWN)
    z1 = order.finish("z1")
    order.start("z1_u", z1, "seq", Y_UP)
    order.start("z1_d", z1, "seq", Y_DOWN)
    far1_u = order.finish("far1_u")
    order.start("far1_f", far1_u, "rep", X_UP)
    far1_d = order.finish("far1_d")
    order.start("z1_c", z1, "seq", C_SWAP)
    far0_f = order.finish("far0_f")
    z1_c = order.finish("z1_c")
    z1_d = order.finish("z1_d")
    order.start("z1_f", z1_d, "seq", Y_DOWN)
    order.start("z1_dc", z1_d, "seq", C_SWAP)
    z1_u = order.finish("z1_u")
    order.start("z1_uc", z1_u, "seq", C_SWAP)
    far1_f = order.finish("far1_f")
    z1_f = order.finish("z1_f")
    order.start("z1_fc", z1_f, "seq", C_SWAP)
    z1_dc, z1_uc, z1_fc = [order.flying.pop(name) for name in ("z1_dc", "z1_uc", "z1_fc")]

    slots = [z_at, z_at ^ 1, jnp.where(z_at < 2, 2, 1), jnp.where(z_at < 2, 3, 0)]
    weights, w_places = [], []
    for z_place, group in zip(slots, (
        (own, own_u, own_d, own_f), (pair, pair_u, pair_d, pair_f),
        (far0, far0_u, far0_d, far0_f), (far1, far1_u, far1_d, far1_f),
    )):
        for hop, block in zip((0, -1, 1, 2), group):
            weights.append(block)
            w_places.append(((x_at + hop) % NX) * ZL + z_place)
    w_places = jnp.stack(w_places).astype(jnp.int32)
    blocks = [away, z1, z1_c, z1_u, z1_uc, z1_d, z1_dc, z1_f, z1_fc]
    unit = rows // 16
    pieces, places = [], [h_at]
    for i in range(NY * NC):
        pieces.append((0, i * early, early))
        places.append(jnp.int32(i * unit))
    for hop in (0, -1, 1, 2):
        for other in range(2):
            pieces.append((len(pieces) - NY * NC + 1, 0, late))
            places.append((((y_at + hop) % NY) * NC + (c_at ^ other)) * unit + early // 16)
    places = jnp.concatenate([jnp.stack(places).astype(jnp.int32), w_places])
    head_output = attend_all(counts, places, near, pieces, blocks, weights)
    attended = lax.all_to_all(head_output, "seq", split_axis=0, concat_axis=1, tiled=True)
    return attended[None]


def solution(mesh):
    in_specs = (
        P("rep", "seq", None),
        P("rep"),
        P("rep"),
        P(),
        P(),
        P("rep", "seq"),
        P("rep", "seq"),
        P("rep", "seq"),
    )
    out_specs = P("rep", "seq", None)
    return jax.shard_map(shards, mesh=mesh, in_specs=in_specs, out_specs=out_specs, check_vma=False)
```
